128 devices in a mesh: dp: 4 (over y), expert: 32 (over x, z, core).
Axes of the slice: x: 4, y: 4, z: 4, core: 2. Of those that a mesh axis runs over, the one named last changes fastest.
Arguments:
- tokens: bfloat16 [16384, 2048], P(('dp', 'expert')), may hold values from -6 to 6
- out_grad: bfloat16 [16384, 2048], P(('dp', 'expert')), may hold values from -3 to 3
- expert_ids: int32 [16384, 4], P(('dp', 'expert')), may hold values from 0 to 127, all different within a row; in each aligned block of 128 rows (0 to 127, 128 to 255, ...) at most 6 rows name the same one
- route_weight: bfloat16 [16384, 4], P(('dp', 'expert')), may hold values from 0.049804688 to 1
- up_weight: bfloat16 [128, 2048, 1536], P(('dp', 'expert')), may hold values from -0.125 to 0.125
- down_weight: bfloat16 [128, 768, 2048], P(('dp', 'expert')), may hold values from -0.21875 to 0.21875
Outputs:
- token_grad: bfloat16 [16384, 2048], P(('dp', 'expert'))
- route_grad: bfloat16 [16384, 4], P(('dp', 'expert'))
- up_grad: bfloat16 [128, 2048, 1536], P(('dp', 'expert'))
- down_grad: bfloat16 [128, 768, 2048], P(('dp', 'expert'))
The draws below stay inside these ranges and needn't reach their ends.
Inputs may be any that keep to these rules, and one draw needn't show every extreme that they name: `expert_ids`: each row names 4 different experts. In the rows of one device no expert is named more than 6 times, and in every draw some device names some expert exactly 6 times.
All inputs are finite; a program needn't handle non-finite values.
Results may differ from the reference program's by a relative error of at most 0.0065.
Values may be sent and summed in bfloat16 or wider, within the bound.
No kernel may reach another device: no remote copies, remote signals or barrier semaphores. Data moves between devices by JAX's collectives and lax.ppermute only.
A program may use at most 128 MiB of HBM per device.

```python
import math
import jax
import jax.numpy as jnp
import numpy as np
from jax import lax

D = 2048
FF = 768
TOP = 4
TOK_DEV = 128
EXPERTS = 128
TOKENS = 16384
CAP = 6


def steps_of(key, dims, shards, least, high):
    def one(axis_at, blocks):
        draws = jax.random.uniform(jax.random.fold_in(jax.random.fold_in(key, 6), axis_at), (blocks,), jnp.float32, least / len(shards), high / len(shards))
        return jnp.repeat(jnp.exp(draws), dims[axis_at] // blocks).reshape((-1,) + (1,) * (len(dims) - axis_at - 1))

    factor_of = one(*shards[0])
    for cut in shards[1:]:
        factor_of = factor_of * one(*cut)
    return factor_of


def shared_out(stream_key, own, number, rows, number_of, top, bound, skew):
    ranking = jax.random.permutation(stream_key, number_of)
    heavy_load, common = portions_of(number_of, rows * top, bound, skew, True), portions_of(number_of, rows * top, bound, skew, False)
    places = jnp.arange(number_of)

    def named(lengths, offset_by):
        used = int((lengths > 0).sum())
        fixed = max(1, used // 4)
        passed = fixed + (places - fixed + offset_by * (used - fixed)) % max(1, number_of - fixed)
        return jnp.zeros((number_of,), jnp.int32).at[ranking[jnp.where(places < fixed, places, passed)]].set(jnp.asarray(lengths, jnp.int32))

    lengths = jnp.where(number % 4 == 0, named(heavy_load, number // 4), named(common, number - number // 4 - 1))
    mixed = jax.random.permutation(jax.random.fold_in(own, 3), number_of)
    source_of, taker = mixed[0:number_of // 2 * 2:2], mixed[1:number_of // 2 * 2:2]
    room = jnp.minimum(lengths[source_of] - 1, bound - lengths[taker]) // 2
    room = jnp.where((source_of == ranking[0]) | (taker == ranking[0]) | (lengths[taker] == 0), 0, jnp.maximum(room, 0))
    passed = jax.random.randint(jax.random.fold_in(own, 4), (number_of // 2,), 0, 1 << 20) % (room + 1)
    lengths = lengths.at[source_of].add(-passed).at[taker].add(passed)
    members = jnp.searchsorted(jnp.cumsum(lengths), jnp.arange(rows * top), side="right").astype(jnp.int32)
    grid = members.reshape(top, rows).T
    grid = grid[jax.random.permutation(jax.random.fold_in(own, 1), rows)]
    offset_by = jax.random.randint(jax.random.fold_in(own, 2), (rows, 1), 0, top)
    return jnp.take_along_axis(grid, (jnp.arange(top)[None, :] + offset_by) % top, axis=1)


def portions_of(number_of, total, reach, skew, full):
    weights = [(1 << 20) // math.isqrt(rank ** skew) + 1 for rank in range(1, number_of + 1)]
    largest = reach if full else min(reach, max(-(-total // number_of), total * weights[0] // sum(weights)))
    least = 1 if total - largest >= number_of - 1 else 0
    holding, spare = [largest] + [least] * (number_of - 1), total - largest - least * (number_of - 1)
    while spare > 0:
        candidates = [i for i in range(1, number_of) if holding[i] < largest] or [i for i in range(1, number_of) if holding[i] < reach]
        pool, left = sum([weights[i] for i in candidates]), spare
        for i in candidates:
            addition = min(reach - holding[i], max(1, left * weights[i] // pool), spare)
            holding[i] = holding[i] + addition
            spare = spare - addition
    return np.array(holding)


def gaussian(stream_key, shape, deviation, reach, split=(), kind=jnp.bfloat16):
    result = jax.random.normal(stream_key, shape, jnp.float32) * deviation
    if len(split) > 0:
        result = steps_of(stream_key, shape, split, -0.22, 0.18) * result
    return jnp.clip(result, min=-reach, max=reach).astype(kind)


def setup_inputs(seed: int = 0) -> dict:
    arg_keys = jax.random.split(jax.random.key(seed), 7)
    tokens = gaussian(arg_keys[0], (TOKENS, D), 1.0, 6.0, ((0, 128),))
    out_grad = gaussian(arg_keys[1], (TOKENS, D), 0.2, 3.0, ((0, 128),))
    expert_ids_keys = jax.random.split(jax.random.fold_in(arg_keys[2], 1), TOKENS // TOK_DEV)
    expert_ids_turns = jax.random.permutation(jax.random.fold_in(arg_keys[2], 3), TOKENS // TOK_DEV)
    expert_ids = jax.vmap(lambda own, number: shared_out(jax.random.fold_in(arg_keys[2], 2), own, number, TOK_DEV, EXPERTS, TOP, CAP, 2))(expert_ids_keys, expert_ids_turns).reshape((TOKENS, TOP))
    route_weight = jnp.clip(jnp.exp(math.log(1.0) - 2.9996462 * jax.random.uniform(arg_keys[3], (TOKENS, TOP), jnp.float32) ** steps_of(arg_keys[3], (TOKENS, TOP), ((0, 128),), -0.2, 0.2)), 0.049804688, 1.0).astype(jnp.bfloat16)
    up_weight = gaussian(arg_keys[4], (EXPERTS, D, 2 * FF), D ** -0.5, 0.125, ((0, 128),))
    down_weight = gaussian(arg_keys[5], (EXPERTS, FF, D), FF ** -0.5, 0.21875, ((0, 128),))
    return {"tokens": tokens, "out_grad": out_grad, "expert_ids": expert_ids, "route_weight": route_weight, "up_weight": up_weight, "down_weight": down_weight}


def silu_parts(gate_pre):
    sigma = jax.nn.sigmoid(gate_pre)
    return gate_pre * sigma, sigma * (1.0 + gate_pre * (1.0 - sigma))


def slot_table(expert_ids):
    blocks = TOKENS // TOK_DEV
    per_block = TOK_DEV * TOP
    flat_ids = expert_ids.reshape(blocks, per_block)
    onehot = (flat_ids[:, :, None] == jnp.arange(EXPERTS, dtype=jnp.int32)[None, None, :]).astype(jnp.int32)
    position = jnp.sum((jnp.cumsum(onehot, axis=1) - 1) * onehot, axis=2).astype(jnp.int32)
    block_index = jnp.broadcast_to(jnp.arange(blocks, dtype=jnp.int32)[:, None], flat_ids.shape)
    assigned = jnp.arange(blocks * per_block, dtype=jnp.int32).reshape(blocks, per_block)
    slot_map = jnp.full((EXPERTS, blocks, CAP), TOKENS * TOP, dtype=jnp.int32)
    return slot_map.at[flat_ids, block_index, position].set(assigned)


def reference(tokens, out_grad, expert_ids, route_weight, up_weight, down_weight):
    slot_map = slot_table(expert_ids)
    zero_row = jnp.zeros((1, D), jnp.bfloat16)
    tok_pad = jnp.concatenate([tokens, zero_row], axis=0)
    grad_pad = jnp.concatenate([out_grad, zero_row], axis=0)
    weight_pad = jnp.concatenate([route_weight.reshape(-1), jnp.zeros((1,), jnp.bfloat16)], axis=0)

    def one_expert(totals, inputs):
        token_acc, route_acc = totals
        slot_rows, up_mat, down_mat = inputs
        flat_index = slot_rows.reshape(-1).astype(jnp.int32)
        token_index = (flat_index // TOP).astype(jnp.int32)
        row_tokens = tok_pad[token_index]
        row_grads = grad_pad[token_index]
        scaled = (weight_pad[flat_index].astype(jnp.float32)[:, None] * row_grads.astype(jnp.float32)).astype(jnp.bfloat16)
        pre_act = jnp.dot(row_tokens, up_mat, preferred_element_type=jnp.float32)
        gate_pre = pre_act[:, :FF]
        up_pre = pre_act[:, FF:]
        gated, derivative = silu_parts(gate_pre)
        hidden = (gated * up_pre).astype(jnp.bfloat16)
        expert_out = jnp.dot(hidden, down_mat, preferred_element_type=jnp.float32)
        slot_route = jnp.sum(row_grads.astype(jnp.float32) * expert_out, axis=1).astype(jnp.bfloat16)
        hid_grad = jnp.dot(scaled, down_mat.T, preferred_element_type=jnp.float32)
        pre_grad = jnp.concatenate([hid_grad * up_pre * derivative, hid_grad * gated], axis=1).astype(jnp.bfloat16)
        slot_grad = jnp.dot(pre_grad, up_mat.T, preferred_element_type=jnp.float32).astype(jnp.bfloat16)
        up_part = jnp.dot(row_tokens.T, pre_grad, preferred_element_type=jnp.float32).astype(jnp.bfloat16)
        down_part = jnp.dot(hidden.T, scaled, preferred_element_type=jnp.float32).astype(jnp.bfloat16)
        token_acc = token_acc.at[token_index].add(slot_grad.astype(jnp.float32))
        route_acc = route_acc.at[flat_index].set(slot_route.astype(jnp.float32))
        return (token_acc, route_acc), (up_part, down_part)

    start = (jnp.zeros((TOKENS + 1, D), jnp.float32), jnp.zeros((TOKENS * TOP + 1,), jnp.float32))
    (token_acc, route_acc), (up_grad, down_grad) = lax.scan(one_expert, start, (slot_map, up_weight, down_weight))
    token_grad = token_acc[:TOKENS].astype(jnp.bfloat16)
    route_grad = route_acc[:TOKENS * TOP].reshape(TOKENS, TOP).astype(jnp.bfloat16)
    return token_grad, route_grad, up_grad, down_grad
```

```python
import jax
import jax.numpy as jnp
from jax import lax
from jax.experimental import pallas as pl
from jax.experimental.pallas import tpu as pltpu
from jax.sharding import PartitionSpec as P

AXES = ("dp", "expert")
TOK = 128
CAP = 6
D = 2048
FF = 768
MAIN = 1536
PIECE = 512
GROUP = 32
F32 = jnp.float32
BF16 = jnp.bfloat16


def dot(a, b):
    return jnp.dot(a, b, preferred_element_type=F32)


def dot_nt(a, b):
    return lax.dot_general(a, b, (((1,), (1,)), ((), ())), preferred_element_type=F32)


def dot_tn(a, b):
    return lax.dot_general(a, b, (((0,), (0,)), ((), ())), preferred_element_type=F32)


def chosen(ids, w):
    expert = lax.broadcasted_iota(jnp.int32, (TOK, TOK), 0)
    token = lax.broadcasted_iota(jnp.int32, (TOK, TOK), 1)
    hot = jnp.zeros((TOK, TOK), F32)
    weight = jnp.zeros((TOK, TOK), F32)
    for k in range(ids.shape[0]):
        named = expert == ids[k : k + 1, :]
        hot = hot + jnp.where(named, 1.0, 0.0)
        weight = weight + jnp.where(named, w[k : k + 1, :], 0.0)
    earlier = jnp.where(expert < token, 1.0, 0.0)
    before = dot(hot.astype(BF16), earlier.astype(BF16))
    return jnp.where(hot > 0.0, before, -9.0), weight


def spread(a):
    return jnp.broadcast_to(a[:, None, :], (a.shape[0], 8, TOK)).reshape(a.shape[0] * 8, TOK)


def slot_of_row(rows, piece):
    r = lax.broadcasted_iota(jnp.int32, (rows, TOK), 0) & 7
    if piece is None:
        return jnp.where(r < CAP, r, -5).astype(F32)
    return jnp.where(r >= CAP, 3 * (r - CAP) + piece, -5).astype(F32)


def dispatch_kernel(ids_ref, w_ref, tok_ref, grad_ref, out_ref, pos_ref, weight_ref, rows_ref):
    step = pl.program_id(0)

    @pl.when(step == 0)
    def _():
        pos, weight = chosen(ids_ref[...], w_ref[...].astype(F32))
        pos_ref[...] = pos
        weight_ref[...] = weight
        for a, ref in enumerate((tok_ref, grad_ref)):
            for j in range(3):
                rows_ref[a, j, :TOK, :] = ref[:, PIECE * j : PIECE * (j + 1)]
                rows_ref[a, j, TOK:, :] = ref[:, MAIN:]

    here = pl.ds(pl.multiple_of(step * GROUP, GROUP), GROUP)
    pos = spread(pos_ref[here, :])
    weight = spread(weight_ref[here, :])
    main = pos == slot_of_row(GROUP * 8, None)
    for j in range(3):
        part = pos == slot_of_row(GROUP * 8, j)
        for a in range(2):
            value = 1.0 if a == 0 else weight
            pick = jnp.concatenate(
                [jnp.where(main, value, 0.0).astype(BF16), jnp.where(part, value, 0.0).astype(BF16)], axis=1
            )
            at = MAIN * a + PIECE * j
            out_ref[:, at : at + PIECE] = dot(pick, rows_ref[a, j]).astype(BF16)


def dispatch(ids, w, tokens, grads):
    whole = lambda shape: pl.BlockSpec(shape, lambda i: (0, 0))
    return pl.pallas_call(
        dispatch_kernel,
        grid=(TOK // GROUP,),
        out_shape=jax.ShapeDtypeStruct((TOK * 8, 2 * MAIN), BF16),
        in_specs=[whole(ids.shape), whole(w.shape), whole(tokens.shape), whole(grads.shape)],
        out_specs=pl.BlockSpec((GROUP * 8, 2 * MAIN), lambda i: (i, 0)),
        scratch_shapes=[
            pltpu.VMEM((TOK, TOK), F32),
            pltpu.VMEM((TOK, TOK), F32),
            pltpu.VMEM((2, 3, 2 * TOK, PIECE), BF16),
        ],
        compiler_params=pltpu.CompilerParams(vmem_limit_bytes=24 * 2**20),
        cost_estimate=pl.CostEstimate(flops=1610612736, bytes_accessed=7340032, transcendentals=0),
        name="dispatch",
    )(ids, w, tokens, grads)


def pack_match(rows, columns, row_axis, piece):
    m = lax.broadcasted_iota(jnp.int32, (rows, columns), row_axis)
    s = lax.broadcasted_iota(jnp.int32, (rows, columns), 1 - row_axis)
    r = m & 7
    first = CAP * (m >> 3)
    if piece is None:
        hit = (s == first + r) & (r < CAP)
    else:
        hit = (s == first + 3 * (r - CAP) + piece) & (r >= CAP)
    return jnp.where(hit, 1.0, 0.0).astype(BF16)


def middle_kernel(
    recv_hbm, up_hbm, down_hbm, x_hbm, s_hbm, hidden_hbm, pre_grad_hbm, back_hbm, route_ref,
    recv, up, down, x, s, hidden, pre_grad, tail, back, in_sem, w_sem, out_sem,
):
    rows, slots = 8 * GROUP, CAP * GROUP
    total = CAP * TOK
    groups = TOK // GROUP
    arrive = [
        pltpu.make_async_copy(recv_hbm.at[pl.ds(rows * g, rows), :], recv.at[pl.ds(rows * g, rows), :], in_sem.at[g])
        for g in range(groups)
    ]
    up_copy = pltpu.make_async_copy(up_hbm, up, w_sem.at[0])
    down_copy = pltpu.make_async_copy(down_hbm, down, w_sem.at[1])
    for c in arrive:
        c.start()
    up_copy.start()
    down_copy.start()
    take = [pack_match(slots, rows, 1, piece) for piece in (None, 0, 1, 2)]
    for g in range(groups):
        arrive[g].wait()
        here = pl.ds(slots * g, slots)
        there = pl.ds(rows * g, rows)
        for a, ref in enumerate((x, s)):
            ref[here, :MAIN] = dot(take[0], recv[there, MAIN * a : MAIN * (a + 1)]).astype(BF16)
            last = jnp.zeros((slots, PIECE), F32)
            for j in range(3):
                at = MAIN * a + PIECE * j
                last = last + dot(take[1 + j], recv[there, at : at + PIECE])
            ref[here, MAIN:] = last.astype(BF16)
    out_x = pltpu.make_async_copy(x, x_hbm, out_sem.at[0])
    out_s = pltpu.make_async_copy(s, s_hbm, out_sem.at[1])
    out_x.start()
    out_s.start()
    up_copy.wait()
    down_copy.wait()
    route = jnp.zeros((total, 1), F32)
    width = 256
    for n in range(FF // width):
        at = width * n
        gate = dot(x[...], up[:, at : at + width])
        lift = dot(x[...], up[:, FF + at : FF + at + width])
        hid_grad = dot_nt(s[...], down[at : at + width, :])
        sigma = jax.nn.sigmoid(gate)
        gated = gate * sigma
        derivative = sigma * (1.0 + gate * (1.0 - sigma))
        hid = (gated * lift).astype(BF16)
        hidden[:, at : at + width] = hid
        route = route + jnp.sum(hid.astype(F32) * hid_grad, axis=1, keepdims=True)
        pre_grad[:, at : at + width] = (hid_grad * lift * derivative).astype(BF16)
        pre_grad[:, FF + at : FF + at + width] = (hid_grad * gated).astype(BF16)
    out_h = pltpu.make_async_copy(hidden, hidden_hbm, out_sem.at[2])
    out_p = pltpu.make_async_copy(pre_grad, pre_grad_hbm, out_sem.at[3])
    out_h.start()
    out_p.start()
    slot = lax.broadcasted_iota(jnp.int32, (total, TOK), 0)
    block = lax.broadcasted_iota(jnp.int32, (total, TOK), 1)
    offset = slot - CAP * block
    for c in range(8):
        route_ref[c : c + 1, :] = jnp.sum(jnp.where((offset == c) & (c < CAP), route, 0.0), axis=0, keepdims=True)
    put = [pack_match(rows, slots, 0, piece) for piece in (None, 0, 1, 2)]
    tail[...] = dot_nt(pre_grad[...], up[MAIN:, :]).astype(BF16)
    leave = []
    for j in range(3):
        at = PIECE * j
        grad = dot_nt(pre_grad[...], up[at : at + PIECE, :]).astype(BF16)
        for g in range(groups):
            packed = dot(put[0], grad[slots * g : slots * (g + 1), :])
            packed = packed + dot(put[1 + j], tail[slots * g : slots * (g + 1), :])
            back[rows * g : rows * (g + 1), at : at + PIECE] = packed.astype(BF16)
        c = pltpu.make_async_copy(
            back.at[:, pl.ds(at, PIECE)], back_hbm.at[:, pl.ds(at, PIECE)], out_sem.at[4 + j]
        )
        c.start()
        leave.append(c)
    for c in [out_x, out_s, out_h, out_p] + leave:
        c.wait()


def middle(recv, up, down):
    total = CAP * TOK
    hbm = pl.BlockSpec(memory_space=pl.ANY)
    shapes = [
        jax.ShapeDtypeStruct((total, D), BF16),
        jax.ShapeDtypeStruct((total, D), BF16),
        jax.ShapeDtypeStruct((total, FF), BF16),
        jax.ShapeDtypeStruct((total, 2 * FF), BF16),
        jax.ShapeDtypeStruct((TOK * 8, MAIN), BF16),
        jax.ShapeDtypeStruct((8, TOK), F32),
    ]
    return pl.pallas_call(
        middle_kernel,
        out_shape=shapes,
        in_specs=[hbm] * 3,
        out_specs=[hbm] * 5 + [pl.BlockSpec(memory_space=pltpu.VMEM)],
        scratch_shapes=[
            pltpu.VMEM((TOK * 8, 2 * MAIN), BF16),
            pltpu.VMEM((D, 2 * FF), BF16),
            pltpu.VMEM((FF, D), BF16),
            pltpu.VMEM((total, D), BF16),
            pltpu.VMEM((total, D), BF16),
            pltpu.VMEM((total, FF), BF16),
            pltpu.VMEM((total, 2 * FF), BF16),
            pltpu.VMEM((total, PIECE), BF16),
            pltpu.VMEM((TOK * 8, MAIN), BF16),
            pltpu.SemaphoreType.DMA((TOK // GROUP,)),
            pltpu.SemaphoreType.DMA((2,)),
            pltpu.SemaphoreType.DMA((7,)),
        ],
        compiler_params=pltpu.CompilerParams(vmem_limit_bytes=56 * 2**20),
        cost_estimate=pl.CostEstimate(flops=16 * 10**9, bytes_accessed=29 * 10**6, transcendentals=589824),
        name="middle",
    )(recv, up, down)


def combine_kernel(me_ref, ids_ref, w_ref, back_ref, sums_ref, token_ref, route_ref):
    ids = ids_ref[...]
    w = w_ref[...].astype(F32)
    pos, _ = chosen(ids, w)
    pos = spread(pos)
    main = pos == slot_of_row(TOK * 8, None)
    last = jnp.zeros((TOK, PIECE), F32)
    for j in range(3):
        part = pos == slot_of_row(TOK * 8, j)
        pick = jnp.concatenate(
            [jnp.where(main, 1.0, 0.0).astype(BF16), jnp.where(part, 1.0, 0.0).astype(BF16)], axis=1
        )
        both = dot_tn(pick, back_ref[:, PIECE * j : PIECE * (j + 1)])
        token_ref[:, PIECE * j : PIECE * (j + 1)] = both[:TOK].astype(BF16)
        last = last + both[TOK:]
    token_ref[:, MAIN:] = last.astype(BF16)
    lane = lax.broadcasted_iota(jnp.int32, (TOK * 8, TOK), 1)
    mine = jnp.sum(jnp.where(lane == me_ref[0], sums_ref[...], 0.0), axis=1, keepdims=True)
    held = jnp.where(main, mine, 0.0)
    expert = lax.broadcasted_iota(jnp.int32, (TOK * 8, TOK), 0) >> 3
    for k in range(ids.shape[0]):
        found = jnp.sum(jnp.where(expert == ids[k : k + 1, :], held, 0.0), axis=0, keepdims=True)
        route_ref[k : k + 1, :] = (found / w[k : k + 1, :]).astype(BF16)


def combine(me, ids, w, back, sums):
    vmem = pl.BlockSpec(memory_space=pltpu.VMEM)
    return pl.pallas_call(
        combine_kernel,
        out_shape=[jax.ShapeDtypeStruct((TOK, D), BF16), jax.ShapeDtypeStruct(ids.shape, BF16)],
        in_specs=[pl.BlockSpec(memory_space=pltpu.SMEM)] + [vmem] * 4,
        out_specs=[vmem] * 2,
        compiler_params=pltpu.CompilerParams(vmem_limit_bytes=24 * 2**20),
        cost_estimate=pl.CostEstimate(flops=805306368, bytes_accessed=4 * 10**6, transcendentals=0),
        name="combine",
    )(me, ids, w, back, sums)


def exchange(a):
    return lax.all_to_all(a, AXES, split_axis=0, concat_axis=0, tiled=True)


def local(tokens, out_grad, expert_ids, route_weight, up_weight, down_weight):
    ids = expert_ids.T
    w = route_weight.T
    send = dispatch(ids, w, tokens, out_grad)
    recv = exchange(send.reshape(TOK, 8, 2 * MAIN)).reshape(TOK * 8, 2 * MAIN)
    x, s, hidden, pre_grad, back, sums = middle(recv, up_weight[0], down_weight[0])
    back = exchange(back.reshape(TOK, 8, MAIN)).reshape(TOK * 8, MAIN)
    sums = lax.all_gather(sums, AXES, axis=0, tiled=True)
    up_grad = dot_tn(x, pre_grad).astype(BF16)[None]
    down_grad = dot_tn(hidden, s).astype(BF16)[None]
    me = (lax.axis_index("dp") * lax.axis_size("expert") + lax.axis_index("expert")).astype(jnp.int32)
    token_grad, route_grad = combine(me.reshape(1), ids, w, back, sums)
    return token_grad, route_grad.T, up_grad, down_grad


def solution(mesh):
    two = P(AXES, None)
    three = P(AXES, None, None)
    return jax.shard_map(
        local,
        mesh=mesh,
        in_specs=(two, two, two, two, three, three),
        out_specs=(two, two, three, three),
        check_vma=False,
    )
```

```python
import jax
import jax.numpy as jnp
from jax import lax
from jax.experimental import pallas as pl
from jax.experimental.pallas import tpu as pltpu
from jax.sharding import PartitionSpec as P

AXES = ("dp", "expert")
TOK = 128
CAP = 6
D = 2048
FF = 768
MAIN = 1536
PIECE = 512
SUMS = 128
GROUP = 32
F32 = jnp.float32
BF16 = jnp.bfloat16


def dot(a, b):
    return jnp.dot(a, b, preferred_element_type=F32)


def dot_nt(a, b):
    return lax.dot_general(a, b, (((1,), (1,)), ((), ())), preferred_element_type=F32)


def dot_tn(a, b):
    return lax.dot_general(a, b, (((0,), (0,)), ((), ())), preferred_element_type=F32)


def chosen(ids, w):
    expert = lax.broadcasted_iota(jnp.int32, (TOK, TOK), 0)
    token = lax.broadcasted_iota(jnp.int32, (TOK, TOK), 1)
    hot = jnp.zeros((TOK, TOK), F32)
    weight = jnp.zeros((TOK, TOK), F32)
    for k in range(ids.shape[0]):
        named = expert == ids[k : k + 1, :]
        hot = hot + jnp.where(named, 1.0, 0.0)
        weight = weight + jnp.where(named, w[k : k + 1, :], 0.0)
    earlier = jnp.where(expert < token, 1.0, 0.0)
    before = dot(hot.astype(BF16), earlier.astype(BF16))
    return jnp.where(hot > 0.0, before, -9.0), weight


def spread(a):
    return jnp.broadcast_to(a[:, None, :], (a.shape[0], 8, TOK)).reshape(a.shape[0] * 8, TOK)


def slot_of_row(rows, piece):
    r = lax.broadcasted_iota(jnp.int32, (rows, TOK), 0) & 7
    if piece is None:
        return jnp.where(r < CAP, r, -5).astype(F32)
    return jnp.where(r >= CAP, 3 * (r - CAP) + piece, -5).astype(F32)


def dispatch_kernel(ids_ref, w_ref, tok_ref, grad_ref, out_ref, pos_ref, weight_ref, rows_ref):
    step = pl.program_id(0)

    @pl.when(step == 0)
    def _():
        pos, weight = chosen(ids_ref[...], w_ref[...].astype(F32))
        pos_ref[...] = pos
        weight_ref[...] = weight
        for a, ref in enumerate((tok_ref, grad_ref)):
            for j in range(3):
                rows_ref[a, j, :TOK, :] = ref[:, PIECE * j : PIECE * (j + 1)]
                rows_ref[a, j, TOK:, :] = ref[:, MAIN:]

    here = pl.ds(pl.multiple_of(step * GROUP, GROUP), GROUP)
    pos = spread(pos_ref[here, :])
    weight = spread(weight_ref[here, :])
    main = pos == slot_of_row(GROUP * 8, None)
    for j in range(3):
        part = pos == slot_of_row(GROUP * 8, j)
        for a in range(2):
            value = 1.0 if a == 0 else weight
            pick = jnp.concatenate(
                [jnp.where(main, value, 0.0).astype(BF16), jnp.where(part, value, 0.0).astype(BF16)], axis=1
            )
            at = MAIN * a + PIECE * j
            out_ref[:, at : at + PIECE] = dot(pick, rows_ref[a, j]).astype(BF16)


def dispatch(ids, w, tokens, grads):
    whole = lambda shape: pl.BlockSpec(shape, lambda i: (0, 0))
    return pl.pallas_call(
        dispatch_kernel,
        grid=(TOK // GROUP,),
        out_shape=jax.ShapeDtypeStruct((TOK * 8, 2 * MAIN), BF16),
        in_specs=[whole(ids.shape), whole(w.shape), whole(tokens.shape), whole(grads.shape)],
        out_specs=pl.BlockSpec((GROUP * 8, 2 * MAIN), lambda i: (i, 0)),
        scratch_shapes=[
            pltpu.VMEM((TOK, TOK), F32),
            pltpu.VMEM((TOK, TOK), F32),
            pltpu.VMEM((2, 3, 2 * TOK, PIECE), BF16),
        ],
        compiler_params=pltpu.CompilerParams(vmem_limit_bytes=56 * 2**20),
        cost_estimate=pl.CostEstimate(flops=1610612736, bytes_accessed=7340032, transcendentals=0),
        name="dispatch",
    )(ids, w, tokens, grads)


def pack_match(rows, columns, row_axis, piece):
    m = lax.broadcasted_iota(jnp.int32, (rows, columns), row_axis)
    s = lax.broadcasted_iota(jnp.int32, (rows, columns), 1 - row_axis)
    r = m & 7
    first = CAP * (m >> 3)
    if piece is None:
        hit = (s == first + r) & (r < CAP)
    else:
        hit = (s == first + 3 * (r - CAP) + piece) & (r >= CAP)
    return jnp.where(hit, 1.0, 0.0).astype(BF16)


def middle_kernel(
    recv_hbm, up_hbm, down_hbm, x_hbm, s_hbm, hidden_hbm, pre_grad_hbm, back_hbm,
    recv, up, down, x, s, hidden, pre_grad, tail, back, in_sem, w_sem, out_sem,
):
    rows, slots = 8 * GROUP, CAP * GROUP
    total = CAP * TOK
    groups = TOK // GROUP
    arrive = [
        pltpu.make_async_copy(recv_hbm.at[pl.ds(rows * g, rows), :], recv.at[pl.ds(rows * g, rows), :], in_sem.at[g])
        for g in range(groups)
    ]
    up_copy = pltpu.make_async_copy(up_hbm, up, w_sem.at[0])
    down_copy = pltpu.make_async_copy(down_hbm, down, w_sem.at[1])
    for c in arrive:
        c.start()
    up_copy.start()
    down_copy.start()
    take = [pack_match(slots, rows, 1, piece) for piece in (None, 0, 1, 2)]
    for g in range(groups):
        arrive[g].wait()
        here = pl.ds(slots * g, slots)
        there = pl.ds(rows * g, rows)
        for a, ref in enumerate((x, s)):
            ref[here, :MAIN] = dot(take[0], recv[there, MAIN * a : MAIN * (a + 1)]).astype(BF16)
            last = jnp.zeros((slots, PIECE), F32)
            for j in range(3):
                at = MAIN * a + PIECE * j
                last = last + dot(take[1 + j], recv[there, at : at + PIECE])
            ref[here, MAIN:] = last.astype(BF16)
    out_x = pltpu.make_async_copy(x, x_hbm, out_sem.at[0])
    out_s = pltpu.make_async_copy(s, s_hbm, out_sem.at[1])
    out_x.start()
    out_s.start()
    up_copy.wait()
    down_copy.wait()
    route = jnp.zeros((total, 1), F32)
    width = 256
    for n in range(FF // width):
        at = width * n
        gate = dot(x[...], up[:, at : at + width])
        lift = dot(x[...], up[:, FF + at : FF + at + width])
        hid_grad = dot_nt(s[...], down[at : at + width, :])
        sigma = jax.nn.sigmoid(gate)
        gated = gate * sigma
        derivative = sigma * (1.0 + gate * (1.0 - sigma))
        hid = (gated * lift).astype(BF16)
        hidden[:, at : at + width] = hid
        route = route + jnp.sum(hid.astype(F32) * hid_grad, axis=1, keepdims=True)
        pre_grad[:, at : at + width] = (hid_grad * lift * derivative).astype(BF16)
        pre_grad[:, FF + at : FF + at + width] = (hid_grad * gated).astype(BF16)
    out_h = pltpu.make_async_copy(hidden, hidden_hbm, out_sem.at[2])
    out_p = pltpu.make_async_copy(pre_grad, pre_grad_hbm, out_sem.at[3])
    out_h.start()
    out_p.start()
    put = [pack_match(rows, slots, 0, piece) for piece in (None, 0, 1, 2)]
    high = route.astype(BF16).astype(F32)
    lane = lax.broadcasted_iota(jnp.int32, (total, SUMS), 1)
    sums = jnp.where(lane == 0, high, jnp.where(lane == 1, route - high, 0.0)).astype(BF16)
    for g in range(groups):
        back[rows * g : rows * (g + 1), MAIN:] = dot(put[0], sums[slots * g : slots * (g + 1), :]).astype(BF16)
    tail[...] = dot_nt(pre_grad[...], up[MAIN:, :]).astype(BF16)
    leave = [pltpu.make_async_copy(back.at[:, pl.ds(MAIN, SUMS)], back_hbm.at[:, pl.ds(MAIN, SUMS)], out_sem.at[7])]
    leave[0].start()
    for j in range(3):
        at = PIECE * j
        grad = dot_nt(pre_grad[...], up[at : at + PIECE, :]).astype(BF16)
        for g in range(groups):
            packed = dot(put[0], grad[slots * g : slots * (g + 1), :])
            packed = packed + dot(put[1 + j], tail[slots * g : slots * (g + 1), :])
            back[rows * g : rows * (g + 1), at : at + PIECE] = packed.astype(BF16)
        c = pltpu.make_async_copy(
            back.at[:, pl.ds(at, PIECE)], back_hbm.at[:, pl.ds(at, PIECE)], out_sem.at[4 + j]
        )
        c.start()
        leave.append(c)
    for c in [out_x, out_s, out_h, out_p] + leave:
        c.wait()


def middle(recv, up, down):
    total = CAP * TOK
    hbm = pl.BlockSpec(memory_space=pl.ANY)
    shapes = [
        jax.ShapeDtypeStruct((total, D), BF16),
        jax.ShapeDtypeStruct((total, D), BF16),
        jax.ShapeDtypeStruct((total, FF), BF16),
        jax.ShapeDtypeStruct((total, 2 * FF), BF16),
        jax.ShapeDtypeStruct((TOK * 8, MAIN + SUMS), BF16),
    ]
    return pl.pallas_call(
        middle_kernel,
        out_shape=shapes,
        in_specs=[hbm] * 3,
        out_specs=[hbm] * 5,
        scratch_shapes=[
            pltpu.VMEM((TOK * 8, 2 * MAIN), BF16),
            pltpu.VMEM((D, 2 * FF), BF16),
            pltpu.VMEM((FF, D), BF16),
            pltpu.VMEM((total, D), BF16),
            pltpu.VMEM((total, D), BF16),
            pltpu.VMEM((total, FF), BF16),
            pltpu.VMEM((total, 2 * FF), BF16),
            pltpu.VMEM((total, PIECE), BF16),
            pltpu.VMEM((TOK * 8, MAIN + SUMS), BF16),
            pltpu.SemaphoreType.DMA((TOK // GROUP,)),
            pltpu.SemaphoreType.DMA((2,)),
            pltpu.SemaphoreType.DMA((8,)),
        ],
        compiler_params=pltpu.CompilerParams(vmem_limit_bytes=56 * 2**20),
        cost_estimate=pl.CostEstimate(flops=16 * 10**9, bytes_accessed=29 * 10**6, transcendentals=589824),
        name="middle",
    )(recv, up, down)


def combine_kernel(ids_ref, w_ref, back_ref, token_ref, route_ref):
    ids = ids_ref[...]
    w = w_ref[...].astype(F32)
    pos, _ = chosen(ids, w)
    pos = spread(pos)
    main = pos == slot_of_row(TOK * 8, None)
    last = jnp.zeros((TOK, PIECE), F32)
    for j in range(3):
        part = pos == slot_of_row(TOK * 8, j)
        pick = jnp.concatenate(
            [jnp.where(main, 1.0, 0.0).astype(BF16), jnp.where(part, 1.0, 0.0).astype(BF16)], axis=1
        )
        both = dot_tn(pick, back_ref[:, PIECE * j : PIECE * (j + 1)])
        token_ref[:, PIECE * j : PIECE * (j + 1)] = both[:TOK].astype(BF16)
        last = last + both[TOK:]
    token_ref[:, MAIN:] = last.astype(BF16)
    mine = jnp.sum(back_ref[:, MAIN:].astype(F32), axis=1, keepdims=True)
    held = jnp.where(main, mine, 0.0)
    expert = lax.broadcasted_iota(jnp.int32, (TOK * 8, TOK), 0) >> 3
    for k in range(ids.shape[0]):
        found = jnp.sum(jnp.where(expert == ids[k : k + 1, :], held, 0.0), axis=0, keepdims=True)
        route_ref[k : k + 1, :] = (found / w[k : k + 1, :]).astype(BF16)


def combine(ids, w, back):
    vmem = pl.BlockSpec(memory_space=pltpu.VMEM)
    return pl.pallas_call(
        combine_kernel,
        out_shape=[jax.ShapeDtypeStruct((TOK, D), BF16), jax.ShapeDtypeStruct(ids.shape, BF16)],
        in_specs=[vmem] * 3,
        out_specs=[vmem] * 2,
        compiler_params=pltpu.CompilerParams(vmem_limit_bytes=24 * 2**20),
        cost_estimate=pl.CostEstimate(flops=805306368, bytes_accessed=4 * 10**6, transcendentals=0),
        name="combine",
    )(ids, w, back)


def exchange(a):
    return lax.all_to_all(a, AXES, split_axis=0, concat_axis=0, tiled=True)


def local(tokens, out_grad, expert_ids, route_weight, up_weight, down_weight):
    ids = expert_ids.T
    w = route_weight.T
    send = dispatch(ids, w, tokens, out_grad)
    recv = exchange(send.reshape(TOK, 8, 2 * MAIN)).reshape(TOK * 8, 2 * MAIN)
    x, s, hidden, pre_grad, back = middle(recv, up_weight[0], down_weight[0])
    back = exchange(back.reshape(TOK, 8, MAIN + SUMS)).reshape(TOK * 8, MAIN + SUMS)
    up_grad = dot_tn(x, pre_grad).astype(BF16)[None]
    down_grad = dot_tn(hidden, s).astype(BF16)[None]
    token_grad, route_grad = combine(ids, w, back)
    return token_grad, route_grad.T, up_grad, down_grad


def solution(mesh):
    two = P(AXES, None)
    three = P(AXES, None, None)
    return jax.shard_map(
        local,
        mesh=mesh,
        in_specs=(two, two, two, two, three, three),
        out_specs=(two, two, three, three),
        check_vma=False,
    )
```

```python
import jax
import jax.numpy as jnp
from jax import lax
from jax.experimental import pallas as pl
from jax.experimental.pallas import tpu as pltpu
from jax.sharding import PartitionSpec as P

AXES = ("dp", "expert")
TOK = 128
CAP = 6
D = 2048
FF = 768
MAIN = 1536
PIECE = 512
SUMS = 128
GROUP = 32
F32 = jnp.float32
BF16 = jnp.bfloat16


def dot(a, b):
    return jnp.dot(a, b, preferred_element_type=F32)


def dot_nt(a, b):
    return lax.dot_general(a, b, (((1,), (1,)), ((), ())), preferred_element_type=F32)


def dot_tn(a, b):
    return lax.dot_general(a, b, (((0,), (0,)), ((), ())), preferred_element_type=F32)


def chosen(ids, w):
    expert = lax.broadcasted_iota(jnp.int32, (TOK, TOK), 0)
    token = lax.broadcasted_iota(jnp.int32, (TOK, TOK), 1)
    hot = jnp.zeros((TOK, TOK), F32)
    weight = jnp.zeros((TOK, TOK), F32)
    for k in range(ids.shape[0]):
        named = expert == ids[k : k + 1, :]
        hot = hot + jnp.where(named, 1.0, 0.0)
        weight = weight + jnp.where(named, w[k : k + 1, :], 0.0)
    earlier = jnp.where(expert < token, 1.0, 0.0)
    before = dot(hot.astype(BF16), earlier.astype(BF16))
    return jnp.where(hot > 0.0, before, -9.0), weight


def spread(a):
    return jnp.broadcast_to(a[:, None, :], (a.shape[0], 8, TOK)).reshape(a.shape[0] * 8, TOK)


def slot_of_row(rows, piece):
    r = lax.broadcasted_iota(jnp.int32, (rows, TOK), 0) & 7
    if piece is None:
        return jnp.where(r < CAP, r, -5).astype(F32)
    return jnp.where(r >= CAP, 3 * (r - CAP) + piece, -5).astype(F32)


def dispatch_kernel(ids_ref, w_ref, tok_ref, grad_ref, out_ref, pos_ref, weight_ref, rows_ref):
    step = pl.program_id(0)

    @pl.when(step == 0)
    def _():
        pos, weight = chosen(ids_ref[...], w_ref[...].astype(F32))
        pos_ref[...] = pos
        weight_ref[...] = weight
        for a, ref in enumerate((tok_ref, grad_ref)):
            for j in range(3):
                rows_ref[a, j, :TOK, :] = ref[:, PIECE * j : PIECE * (j + 1)]
                rows_ref[a, j, TOK:, :] = ref[:, MAIN:]

    here = pl.ds(pl.multiple_of(step * GROUP, GROUP), GROUP)
    pos = spread(pos_ref[here, :])
    weight = spread(weight_ref[here, :])
    main = pos == slot_of_row(GROUP * 8, None)
    for j in range(3):
        part = pos == slot_of_row(GROUP * 8, j)
        for a in range(2):
            value = 1.0 if a == 0 else weight
            pick = jnp.concatenate(
                [jnp.where(main, value, 0.0).astype(BF16), jnp.where(part, value, 0.0).astype(BF16)], axis=1
            )
            at = MAIN * a + PIECE * j
            out_ref[:, at : at + PIECE] = dot(pick, rows_ref[a, j]).astype(BF16)


def dispatch(ids, w, tokens, grads):
    whole = lambda shape: pl.BlockSpec(shape, lambda i: (0, 0))
    return pl.pallas_call(
        dispatch_kernel,
        grid=(TOK // GROUP,),
        out_shape=jax.ShapeDtypeStruct((TOK * 8, 2 * MAIN), BF16),
        in_specs=[whole(ids.shape), whole(w.shape), whole(tokens.shape), whole(grads.shape)],
        out_specs=pl.BlockSpec((GROUP * 8, 2 * MAIN), lambda i: (i, 0)),
        scratch_shapes=[
            pltpu.VMEM((TOK, TOK), F32),
            pltpu.VMEM((TOK, TOK), F32),
            pltpu.VMEM((2, 3, 2 * TOK, PIECE), BF16),
        ],
        compiler_params=pltpu.CompilerParams(vmem_limit_bytes=56 * 2**20),
        cost_estimate=pl.CostEstimate(flops=1610612736, bytes_accessed=7340032, transcendentals=0),
        name="dispatch",
    )(ids, w, tokens, grads)


def pack_match(rows, columns, row_axis, piece):
    m = lax.broadcasted_iota(jnp.int32, (rows, columns), row_axis)
    s = lax.broadcasted_iota(jnp.int32, (rows, columns), 1 - row_axis)
    r = m & 7
    first = CAP * (m >> 3)
    if piece is None:
        hit = (s == first + r) & (r < CAP)
    else:
        hit = (s == first + 3 * (r - CAP) + piece) & (r >= CAP)
    return jnp.where(hit, 1.0, 0.0).astype(BF16)


def middle_kernel(
    recv_hbm, up_hbm, down_hbm, x_hbm, s_hbm, hidden_hbm, pre_grad_hbm, back_hbm,
    recv, up, down, x, s, hidden, pre_grad, tail, back, in_sem, w_sem, out_sem,
):
    rows, slots = 8 * GROUP, CAP * GROUP
    total = CAP * TOK
    groups = TOK // GROUP
    arrive = [
        pltpu.make_async_copy(recv_hbm.at[pl.ds(rows * g, rows), :], recv.at[pl.ds(rows * g, rows), :], in_sem.at[g])
        for g in range(groups)
    ]
    up_copy = pltpu.make_async_copy(up_hbm, up, w_sem.at[0])
    down_copy = pltpu.make_async_copy(down_hbm, down, w_sem.at[1])
    for c in arrive:
        c.start()
    up_copy.start()
    down_copy.start()
    take = [pack_match(slots, rows, 1, piece) for piece in (None, 0, 1, 2)]
    for g in range(groups):
        arrive[g].wait()
        here = pl.ds(slots * g, slots)
        there = pl.ds(rows * g, rows)
        for a, ref in enumerate((x, s)):
            ref[here, :MAIN] = dot(take[0], recv[there, MAIN * a : MAIN * (a + 1)]).astype(BF16)
            last = jnp.zeros((slots, PIECE), F32)
            for j in range(3):
                at = MAIN * a + PIECE * j
                last = last + dot(take[1 + j], recv[there, at : at + PIECE])
            ref[here, MAIN:] = last.astype(BF16)
    out_x = pltpu.make_async_copy(x, x_hbm, out_sem.at[0])
    out_s = pltpu.make_async_copy(s, s_hbm, out_sem.at[1])
    up_copy.wait()
    down_copy.wait()
    width, height = 256, 384
    shares = [jnp.zeros((height, SUMS), F32) for _ in range(total // height)]

    def finish(n, m, gate, lift, hid_grad):
        here, at = slice(height * m, height * (m + 1)), width * n
        sigma = 0.5 * jnp.tanh(0.5 * gate) + 0.5
        gated = gate * sigma
        derivative = sigma + gated * (1.0 - sigma)
        hid = (gated * lift).astype(BF16)
        hidden[here, at : at + width] = hid
        pre_grad[here, at : at + width] = (hid_grad * lift * derivative).astype(BF16)
        pre_grad[here, FF + at : FF + at + width] = (hid_grad * gated).astype(BF16)
        share = hid.astype(F32) * hid_grad
        for i in range(0, width, SUMS):
            shares[m] = shares[m] + share[:, i : i + SUMS]

    waiting = None
    for n in range(FF // width):
        at = width * n
        for m in range(total // height):
            here = slice(height * m, height * (m + 1))
            made = (
                n,
                m,
                dot(x[here, :], up[:, at : at + width]),
                dot(x[here, :], up[:, FF + at : FF + at + width]),
                dot_nt(s[here, :], down[at : at + width, :]),
            )
            if waiting is not None:
                finish(*waiting)
            waiting = made
    finish(*waiting)
    route = jnp.concatenate(shares, axis=0)
    out_x.start()
    out_s.start()
    out_h = pltpu.make_async_copy(hidden, hidden_hbm, out_sem.at[2])
    out_p = pltpu.make_async_copy(pre_grad, pre_grad_hbm, out_sem.at[3])
    out_h.start()
    out_p.start()
    put = [pack_match(rows, slots, 0, piece) for piece in (None, 0, 1, 2)]
    route = jnp.sum(route, axis=1, keepdims=True)
    high = route.astype(BF16).astype(F32)
    lane = lax.broadcasted_iota(jnp.int32, (total, SUMS), 1)
    sums = jnp.where(lane == 0, high, jnp.where(lane == 1, route - high, 0.0)).astype(BF16)
    for g in range(groups):
        back[rows * g : rows * (g + 1), MAIN:] = dot(put[0], sums[slots * g : slots * (g + 1), :]).astype(BF16)
    tail[...] = dot_nt(pre_grad[...], up[MAIN:, :]).astype(BF16)
    leave = [pltpu.make_async_copy(back.at[:, pl.ds(MAIN, SUMS)], back_hbm.at[:, pl.ds(MAIN, SUMS)], out_sem.at[7])]
    leave[0].start()
    for j in range(3):
        at = PIECE * j
        grad = dot_nt(pre_grad[...], up[at : at + PIECE, :]).astype(BF16)
        for g in range(groups):
            packed = dot(put[0], grad[slots * g : slots * (g + 1), :])
            packed = packed + dot(put[1 + j], tail[slots * g : slots * (g + 1), :])
            back[rows * g : rows * (g + 1), at : at + PIECE] = packed.astype(BF16)
        c = pltpu.make_async_copy(
            back.at[:, pl.ds(at, PIECE)], back_hbm.at[:, pl.ds(at, PIECE)], out_sem.at[4 + j]
        )
        c.start()
        leave.append(c)
    for c in [out_x, out_s, out_h, out_p] + leave:
        c.wait()


def middle(recv, up, down):
    total = CAP * TOK
    hbm = pl.BlockSpec(memory_space=pl.ANY)
    shapes = [
        jax.ShapeDtypeStruct((total, D), BF16),
        jax.ShapeDtypeStruct((total, D), BF16),
        jax.ShapeDtypeStruct((total, FF), BF16),
        jax.ShapeDtypeStruct((total, 2 * FF), BF16),
        jax.ShapeDtypeStruct((TOK * 8, MAIN + SUMS), BF16),
    ]
    return pl.pallas_call(
        middle_kernel,
        out_shape=shapes,
        in_specs=[hbm] * 3,
        out_specs=[hbm] * 5,
        scratch_shapes=[
            pltpu.VMEM((TOK * 8, 2 * MAIN), BF16),
            pltpu.VMEM((D, 2 * FF), BF16),
            pltpu.VMEM((FF, D), BF16),
            pltpu.VMEM((total, D), BF16),
            pltpu.VMEM((total, D), BF16),
            pltpu.VMEM((total, FF), BF16),
            pltpu.VMEM((total, 2 * FF), BF16),
            pltpu.VMEM((total, PIECE), BF16),
            pltpu.VMEM((TOK * 8, MAIN + SUMS), BF16),
            pltpu.SemaphoreType.DMA((TOK // GROUP,)),
            pltpu.SemaphoreType.DMA((2,)),
            pltpu.SemaphoreType.DMA((8,)),
        ],
        compiler_params=pltpu.CompilerParams(vmem_limit_bytes=56 * 2**20),
        cost_estimate=pl.CostEstimate(flops=16 * 10**9, bytes_accessed=29 * 10**6, transcendentals=589824),
        name="middle",
    )(recv, up, down)


def combine_kernel(ids_ref, w_ref, back_ref, token_ref, route_ref):
    ids = ids_ref[...]
    w = w_ref[...].astype(F32)
    pos, _ = chosen(ids, w)
    pos = spread(pos)
    main = pos == slot_of_row(TOK * 8, None)
    last = jnp.zeros((TOK, PIECE), F32)
    for j in range(3):
        part = pos == slot_of_row(TOK * 8, j)
        pick = jnp.concatenate(
            [jnp.where(main, 1.0, 0.0).astype(BF16), jnp.where(part, 1.0, 0.0).astype(BF16)], axis=1
        )
        both = dot_tn(pick, back_ref[:, PIECE * j : PIECE * (j + 1)])
        token_ref[:, PIECE * j : PIECE * (j + 1)] = both[:TOK].astype(BF16)
        last = last + both[TOK:]
    token_ref[:, MAIN:] = last.astype(BF16)
    mine = jnp.sum(back_ref[:, MAIN:].astype(F32), axis=1, keepdims=True)
    held = jnp.where(main, mine, 0.0)
    expert = lax.broadcasted_iota(jnp.int32, (TOK * 8, TOK), 0) >> 3
    for k in range(ids.shape[0]):
        found = jnp.sum(jnp.where(expert == ids[k : k + 1, :], held, 0.0), axis=0, keepdims=True)
        route_ref[k : k + 1, :] = (found / w[k : k + 1, :]).astype(BF16)


def combine(ids, w, back):
    vmem = pl.BlockSpec(memory_space=pltpu.VMEM)
    return pl.pallas_call(
        combine_kernel,
        out_shape=[jax.ShapeDtypeStruct((TOK, D), BF16), jax.ShapeDtypeStruct(ids.shape, BF16)],
        in_specs=[vmem] * 3,
        out_specs=[vmem] * 2,
        compiler_params=pltpu.CompilerParams(vmem_limit_bytes=24 * 2**20),
        cost_estimate=pl.CostEstimate(flops=805306368, bytes_accessed=4 * 10**6, transcendentals=0),
        name="combine",
    )(ids, w, back)


def exchange(a):
    return lax.all_to_all(a, AXES, split_axis=0, concat_axis=0, tiled=True)


def local(tokens, out_grad, expert_ids, route_weight, up_weight, down_weight):
    ids = expert_ids.T
    w = route_weight.T
    send = dispatch(ids, w, tokens, out_grad)
    recv = exchange(send.reshape(TOK, 8, 2 * MAIN)).reshape(TOK * 8, 2 * MAIN)
    x, s, hidden, pre_grad, back = middle(recv, up_weight[0], down_weight[0])
    back = exchange(back.reshape(TOK, 8, MAIN + SUMS)).reshape(TOK * 8, MAIN + SUMS)
    up_grad = dot_tn(x, pre_grad).astype(BF16)[None]
    down_grad = dot_tn(hidden, s).astype(BF16)[None]
    token_grad, route_grad = combine(ids, w, back)
    return token_grad, route_grad.T, up_grad, down_grad


def solution(mesh):
    two = P(AXES, None)
    three = P(AXES, None, None)
    return jax.shard_map(
        local,
        mesh=mesh,
        in_specs=(two, two, two, two, three, three),
        out_specs=(two, two, three, three),
        check_vma=False,
    )
```

```python
import jax
import jax.numpy as jnp
from jax import lax
from jax.experimental import pallas as pl
from jax.experimental.pallas import tpu as pltpu
from jax.sharding import PartitionSpec as P

AXES = ("dp", "expert")
TOK = 128
CAP = 6
D = 2048
FF = 768
MAIN = 1536
PIECE = 512
SUMS = 128
GROUP = 32
STEP = 16
F32 = jnp.float32
BF16 = jnp.bfloat16


def dot(a, b):
    return jnp.dot(a, b, preferred_element_type=F32)


def dot_nt(a, b):
    return lax.dot_general(a, b, (((1,), (1,)), ((), ())), preferred_element_type=F32)


def dot_tn(a, b):
    return lax.dot_general(a, b, (((0,), (0,)), ((), ())), preferred_element_type=F32)


def chosen(ids, w):
    expert = lax.broadcasted_iota(jnp.int32, (TOK, TOK), 0)
    token = lax.broadcasted_iota(jnp.int32, (TOK, TOK), 1)
    hot = jnp.zeros((TOK, TOK), F32)
    weight = jnp.zeros((TOK, TOK), F32)
    for k in range(ids.shape[0]):
        named = expert == ids[k : k + 1, :]
        hot = hot + jnp.where(named, 1.0, 0.0)
        weight = weight + jnp.where(named, w[k : k + 1, :], 0.0)
    earlier = jnp.where(expert < token, 1.0, 0.0)
    before = dot(hot.astype(BF16), earlier.astype(BF16))
    return jnp.where(hot > 0.0, before, -9.0), weight


def spread(a):
    return jnp.broadcast_to(a[:, None, :], (a.shape[0], 8, TOK)).reshape(a.shape[0] * 8, TOK)


def slot_of_row(rows, piece):
    r = lax.broadcasted_iota(jnp.int32, (rows, TOK), 0) & 7
    if piece is None:
        return jnp.where(r < CAP, r, -5).astype(F32)
    return jnp.where(r >= CAP, 3 * (r - CAP) + piece, -5).astype(F32)


def dispatch_kernel(ids_ref, w_ref, tok_ref, grad_ref, out_ref, pos_ref, weight_ref, rows_ref):
    step = pl.program_id(0)

    @pl.when(step == 0)
    def _():
        pos, weight = chosen(ids_ref[...], w_ref[...].astype(F32))
        pos_ref[...] = pos
        weight_ref[...] = weight
        for a, ref in enumerate((tok_ref, grad_ref)):
            for j in range(3):
                rows_ref[a, j, :TOK, :] = ref[:, PIECE * j : PIECE * (j + 1)]
                rows_ref[a, j, TOK:, :] = ref[:, MAIN:]

    here = pl.ds(pl.multiple_of(step * STEP, STEP), STEP)
    pos = spread(pos_ref[here, :])
    weight = spread(weight_ref[here, :])
    main = pos == slot_of_row(STEP * 8, None)
    for j in range(3):
        part = pos == slot_of_row(STEP * 8, j)
        for a in range(2):
            value = 1.0 if a == 0 else weight
            pick = jnp.concatenate(
                [jnp.where(main, value, 0.0).astype(BF16), jnp.where(part, value, 0.0).astype(BF16)], axis=1
            )
            at = MAIN * a + PIECE * j
            out_ref[:, at : at + PIECE] = dot(pick, rows_ref[a, j]).astype(BF16)


def dispatch(ids, w, tokens, grads):
    whole = lambda shape: pl.BlockSpec(shape, lambda i: (0, 0))
    return pl.pallas_call(
        dispatch_kernel,
        grid=(TOK // STEP,),
        out_shape=jax.ShapeDtypeStruct((TOK * 8, 2 * MAIN), BF16),
        in_specs=[whole(ids.shape), whole(w.shape), whole(tokens.shape), whole(grads.shape)],
        out_specs=pl.BlockSpec((STEP * 8, 2 * MAIN), lambda i: (i, 0)),
        scratch_shapes=[
            pltpu.VMEM((TOK, TOK), F32),
            pltpu.VMEM((TOK, TOK), F32),
            pltpu.VMEM((2, 3, 2 * TOK, PIECE), BF16),
        ],
        compiler_params=pltpu.CompilerParams(vmem_limit_bytes=56 * 2**20),
        cost_estimate=pl.CostEstimate(flops=1610612736, bytes_accessed=7340032, transcendentals=0),
        name="dispatch",
    )(ids, w, tokens, grads)


def pack_match(rows, columns, row_axis, piece):
    m = lax.broadcasted_iota(jnp.int32, (rows, columns), row_axis)
    s = lax.broadcasted_iota(jnp.int32, (rows, columns), 1 - row_axis)
    r = m & 7
    first = CAP * (m >> 3)
    if piece is None:
        hit = (s == first + r) & (r < CAP)
    else:
        hit = (s == first + 3 * (r - CAP) + piece) & (r >= CAP)
    return jnp.where(hit, 1.0, 0.0).astype(BF16)


def middle_kernel(
    recv_hbm, up_hbm, down_hbm, x_hbm, s_hbm, hidden_hbm, pre_grad_hbm, back_hbm,
    recv, up, down, x, s, hidden, pre_grad, tail, back, in_sem, w_sem, out_sem,
):
    rows, slots = 8 * GROUP, CAP * GROUP
    total = CAP * TOK
    groups = TOK // GROUP
    arrive = [
        pltpu.make_async_copy(recv_hbm.at[pl.ds(rows * g, rows), :], recv.at[pl.ds(rows * g, rows), :], in_sem.at[g])
        for g in range(groups)
    ]
    up_copy = pltpu.make_async_copy(up_hbm, up, w_sem.at[0])
    down_copy = pltpu.make_async_copy(down_hbm, down, w_sem.at[1])
    for c in arrive:
        c.start()
    up_copy.start()
    down_copy.start()
    take = [pack_match(slots, rows, 1, piece) for piece in (None, 0, 1, 2)]
    for g in range(groups):
        arrive[g].wait()
        here = pl.ds(slots * g, slots)
        there = pl.ds(rows * g, rows)
        for a, ref in enumerate((x, s)):
            ref[here, :MAIN] = dot(take[0], recv[there, MAIN * a : MAIN * (a + 1)]).astype(BF16)
            last = jnp.zeros((slots, PIECE), F32)
            for j in range(3):
                at = MAIN * a + PIECE * j
                last = last + dot(take[1 + j], recv[there, at : at + PIECE])
            ref[here, MAIN:] = last.astype(BF16)
    out_x = pltpu.make_async_copy(x, x_hbm, out_sem.at[0])
    out_s = pltpu.make_async_copy(s, s_hbm, out_sem.at[1])
    up_copy.wait()
    down_copy.wait()
    width, height = 256, 384
    shares = [jnp.zeros((height, SUMS), F32) for _ in range(total // height)]

    def finish(n, m, gate, lift, hid_grad):
        here, at = slice(height * m, height * (m + 1)), width * n
        sigma = 0.5 * jnp.tanh(0.5 * gate) + 0.5
        gated = gate * sigma
        derivative = sigma + gated * (1.0 - sigma)
        hid = (gated * lift).astype(BF16)
        hidden[here, at : at + width] = hid
        pre_grad[here, at : at + width] = (hid_grad * lift * derivative).astype(BF16)
        pre_grad[here, FF + at : FF + at + width] = (hid_grad * gated).astype(BF16)
        share = hid.astype(F32) * hid_grad
        for i in range(0, width, SUMS):
            shares[m] = shares[m] + share[:, i : i + SUMS]

    waiting = None
    for n in range(FF // width):
        at = width * n
        for m in range(total // height):
            here = slice(height * m, height * (m + 1))
            made = (
                n,
                m,
                dot(x[here, :], up[:, at : at + width]),
                dot(x[here, :], up[:, FF + at : FF + at + width]),
                dot_nt(s[here, :], down[at : at + width, :]),
            )
            if waiting is not None:
                finish(*waiting)
            waiting = made
    finish(*waiting)
    route = jnp.concatenate(shares, axis=0)
    out_x.start()
    out_s.start()
    out_h = pltpu.make_async_copy(hidden, hidden_hbm, out_sem.at[2])
    out_p = pltpu.make_async_copy(pre_grad, pre_grad_hbm, out_sem.at[3])
    out_h.start()
    out_p.start()
    put = [pack_match(rows, slots, 0, piece) for piece in (None, 0, 1, 2)]
    route = jnp.sum(route, axis=1, keepdims=True)
    high = route.astype(BF16).astype(F32)
    lane = lax.broadcasted_iota(jnp.int32, (total, SUMS), 1)
    sums = jnp.where(lane == 0, high, jnp.where(lane == 1, route - high, 0.0)).astype(BF16)
    for g in range(groups):
        back[rows * g : rows * (g + 1), MAIN:] = dot(put[0], sums[slots * g : slots * (g + 1), :]).astype(BF16)
    tail[...] = dot_nt(pre_grad[...], up[MAIN:, :]).astype(BF16)
    leave = [pltpu.make_async_copy(back.at[:, pl.ds(MAIN, SUMS)], back_hbm.at[:, pl.ds(MAIN, SUMS)], out_sem.at[7])]
    leave[0].start()
    for j in range(3):
        at = PIECE * j
        grad = dot_nt(pre_grad[...], up[at : at + PIECE, :]).astype(BF16)
        for g in range(groups):
            packed = dot(put[0], grad[slots * g : slots * (g + 1), :])
            packed = packed + dot(put[1 + j], tail[slots * g : slots * (g + 1), :])
            back[rows * g : rows * (g + 1), at : at + PIECE] = packed.astype(BF16)
        c = pltpu.make_async_copy(
            back.at[:, pl.ds(at, PIECE)], back_hbm.at[:, pl.ds(at, PIECE)], out_sem.at[4 + j]
        )
        c.start()
        leave.append(c)
    for c in [out_x, out_s, out_h, out_p] + leave:
        c.wait()


def middle(recv, up, down):
    total = CAP * TOK
    hbm = pl.BlockSpec(memory_space=pl.ANY)
    shapes = [
        jax.ShapeDtypeStruct((total, D), BF16),
        jax.ShapeDtypeStruct((total, D), BF16),
        jax.ShapeDtypeStruct((total, FF), BF16),
        jax.ShapeDtypeStruct((total, 2 * FF), BF16),
        jax.ShapeDtypeStruct((TOK * 8, MAIN + SUMS), BF16),
    ]
    return pl.pallas_call(
        middle_kernel,
        out_shape=shapes,
        in_specs=[hbm] * 3,
        out_specs=[hbm] * 5,
        scratch_shapes=[
            pltpu.VMEM((TOK * 8, 2 * MAIN), BF16),
            pltpu.VMEM((D, 2 * FF), BF16),
            pltpu.VMEM((FF, D), BF16),
            pltpu.VMEM((total, D), BF16),
            pltpu.VMEM((total, D), BF16),
            pltpu.VMEM((total, FF), BF16),
            pltpu.VMEM((total, 2 * FF), BF16),
            pltpu.VMEM((total, PIECE), BF16),
            pltpu.VMEM((TOK * 8, MAIN + SUMS), BF16),
            pltpu.SemaphoreType.DMA((TOK // GROUP,)),
            pltpu.SemaphoreType.DMA((2,)),
            pltpu.SemaphoreType.DMA((8,)),
        ],
        compiler_params=pltpu.CompilerParams(vmem_limit_bytes=56 * 2**20),
        cost_estimate=pl.CostEstimate(flops=16 * 10**9, bytes_accessed=29 * 10**6, transcendentals=589824),
        name="middle",
    )(recv, up, down)


def combine_kernel(ids_ref, w_ref, back_ref, token_ref, route_ref):
    ids = ids_ref[...]
    w = w_ref[...].astype(F32)
    pos, _ = chosen(ids, w)
    pos = spread(pos)
    main = pos == slot_of_row(TOK * 8, None)
    last = jnp.zeros((TOK, PIECE), F32)
    for j in range(3):
        part = pos == slot_of_row(TOK * 8, j)
        pick = jnp.concatenate(
            [jnp.where(main, 1.0, 0.0).astype(BF16), jnp.where(part, 1.0, 0.0).astype(BF16)], axis=1
        )
        both = dot_tn(pick, back_ref[:, PIECE * j : PIECE * (j + 1)])
        token_ref[:, PIECE * j : PIECE * (j + 1)] = both[:TOK].astype(BF16)
        last = last + both[TOK:]
    token_ref[:, MAIN:] = last.astype(BF16)
    mine = jnp.sum(back_ref[:, MAIN:].astype(F32), axis=1, keepdims=True)
    held = jnp.where(main, mine, 0.0)
    expert = lax.broadcasted_iota(jnp.int32, (TOK * 8, TOK), 0) >> 3
    for k in range(ids.shape[0]):
        found = jnp.sum(jnp.where(expert == ids[k : k + 1, :], held, 0.0), axis=0, keepdims=True)
        route_ref[k : k + 1, :] = (found / w[k : k + 1, :]).astype(BF16)


def combine(ids, w, back):
    vmem = pl.BlockSpec(memory_space=pltpu.VMEM)
    return pl.pallas_call(
        combine_kernel,
        out_shape=[jax.ShapeDtypeStruct((TOK, D), BF16), jax.ShapeDtypeStruct(ids.shape, BF16)],
        in_specs=[vmem] * 3,
        out_specs=[vmem] * 2,
        compiler_params=pltpu.CompilerParams(vmem_limit_bytes=24 * 2**20),
        cost_estimate=pl.CostEstimate(flops=805306368, bytes_accessed=4 * 10**6, transcendentals=0),
        name="combine",
    )(ids, w, back)


def exchange(a):
    return lax.all_to_all(a, AXES, split_axis=0, concat_axis=0, tiled=True)


def local(tokens, out_grad, expert_ids, route_weight, up_weight, down_weight):
    ids = expert_ids.T
    w = route_weight.T
    send = dispatch(ids, w, tokens, out_grad)
    recv = exchange(send.reshape(TOK, 8, 2 * MAIN)).reshape(TOK * 8, 2 * MAIN)
    x, s, hidden, pre_grad, back = middle(recv, up_weight[0], down_weight[0])
    back = exchange(back.reshape(TOK, 8, MAIN + SUMS)).reshape(TOK * 8, MAIN + SUMS)
    up_grad = dot_tn(x, pre_grad).astype(BF16)[None]
    down_grad = dot_tn(hidden, s).astype(BF16)[None]
    token_grad, route_grad = combine(ids, w, back)
    return token_grad, route_grad.T, up_grad, down_grad


def solution(mesh):
    two = P(AXES, None)
    three = P(AXES, None, None)
    return jax.shard_map(
        local,
        mesh=mesh,
        in_specs=(two, two, two, two, three, three),
        out_specs=(two, two, three, three),
        check_vma=False,
    )
```
